32 devices in a mesh: runs: 2 (over y), shot: 4 (over x, core), slab: 4 (over z).
Axes of the slice: x: 2, y: 2, z: 4, core: 2. Of those that a mesh axis runs over, the one named last changes fastest.
Arguments:
- source_now: float32 [16, 64, 16, 256], P(('runs', 'shot'), 'slab'), parts along dimension 0, may hold values from -4 to 4
- source_prev: float32 [16, 64, 16, 256], P(('runs', 'shot'), 'slab'), parts along dimension 0, may hold values from -4 to 4
- receiver_now: float32 [16, 64, 16, 256], P(('runs', 'shot'), 'slab'), parts along dimension 0, may hold values from -4 to 4
- receiver_prev: float32 [16, 64, 16, 256], P(('runs', 'shot'), 'slab'), parts along dimension 0, may hold values from -4 to 4
- courant_sq: float32 [128, 16, 256], P(('runs', 'slab')), parts along dimension 0, may hold values from 0.26 to 0.52
- source_cell: int32 [16], P(('runs', 'shot')), parts along dimension 0, may hold values from 0 to 1023
- wavelet: float32 [8, 16], P(None, ('runs', 'shot')), parts along dimension 1, may hold values from -12 to 12
- receiver_cell: int32 [16, 256], P(('runs', 'shot')), parts along dimension 0, may hold values from 0 to 1023
- traces: float32 [8, 16, 256], P(None, ('runs', 'shot')), parts along dimension 1, may hold values from -10 to 10
- offset_perm: int32 [16], P('runs'), parts along dimension 0, may hold values from 0 to 7, each once
Outputs:
- offset_image: float32 [16, 64, 16, 256], P(('runs', 'shot'), 'slab'), parts along dimension 0
- source_final: float32 [16, 64, 16, 256], P(('runs', 'shot'), 'slab'), parts along dimension 0
- receiver_final: float32 [16, 64, 16, 256], P(('runs', 'shot'), 'slab'), parts along dimension 0
The draws below stay inside these ranges and needn't reach their ends.
There are 2 independent parts, one for each index of `runs`. The reference program is written for one: setup_inputs(seed, part) draws one part's arguments, and reference() takes and returns one part's arrays. A program takes and returns all parts, laid end to end along the dimension named above; each array names one. Nothing has to cross between parts.
Inputs may be any that keep to these rules, and one draw needn't show every extreme that they name: `source_cell`: a surface cell index. `receiver_cell`: surface cell indices; two receivers may share a cell. `offset_perm`: every offset index appears once.
All inputs are finite; a program needn't handle non-finite values.
Results may differ from the reference program's by a relative error of at most 0.0003.
Values sent between devices are 32-bit elements; how exact they have to be, the bound alone decides.
A program may use at most 64 MiB of HBM per device.

```python
import math
import jax
import jax.numpy as jnp
from jax import lax

NY = 16
NZ = 256
RECV = 256
STEPS = 8
INJECT_Z = 4
NX = 64
SHOTS = 8
OFFSETS = 8


def with_ends(values, own_key, smallest, high):
    place = [jax.random.randint(jax.random.fold_in(own_key, axis), (), 0, length) for axis, length in enumerate(values.shape)]
    widest = values.shape.index(max(values.shape))
    next_to = place[:widest] + [(place[widest] + 1) % values.shape[widest]] + place[widest + 1:]
    return values.at[tuple(place)].set(smallest).at[tuple(next_to)].set(high)


def block_scale(stream_key, dims, split, least, largest):
    level, own = 1.0, jax.random.fold_in(stream_key, 6)
    for position, shards_of in split:
        steps = jnp.exp(jax.random.uniform(jax.random.fold_in(own, position), (shards_of,), jnp.float32, least / len(split), largest / len(split)))
        level = level * jnp.repeat(steps, dims[position] // shards_of).reshape([-1 if axis == position else 1 for axis in range(len(dims))])
    return level


def noise(own_key, extent, scale, reach, cuts=(), kind=jnp.bfloat16):
    entries = scale * jax.random.normal(own_key, extent, jnp.float32)
    if cuts:
        entries = entries * block_scale(own_key, extent, cuts, -0.22, 0.18)
    return jnp.clip(entries, -reach, reach).astype(kind)


def setup_inputs(seed: int = 0, part: int = 0) -> dict:
    keys = jax.random.split(jax.random.key(seed), 11)
    part_keys = jax.random.split(jax.random.fold_in(keys[10], part), 11)
    source_now = noise(part_keys[0], (SHOTS, NX, NY, NZ), 0.5, 4.0, ((0, 4), (1, 4)), jnp.float32)
    source_prev = noise(part_keys[1], (SHOTS, NX, NY, NZ), 0.5, 4.0, ((0, 4), (1, 4)), jnp.float32)
    receiver_now = noise(part_keys[2], (SHOTS, NX, NY, NZ), 0.5, 4.0, ((0, 4), (1, 4)), jnp.float32)
    receiver_prev = noise(part_keys[3], (SHOTS, NX, NY, NZ), 0.5, 4.0, ((0, 4), (1, 4)), jnp.float32)
    courant_sq = jnp.clip(jnp.exp(math.log(0.52) - 0.6931472 * jax.random.uniform(part_keys[4], (NX, NY, NZ), jnp.float32) ** block_scale(part_keys[4], (NX, NY, NZ), ((0, 4),), -0.2, 0.2)), 0.26, 0.52)
    source_cell = with_ends(jax.random.randint(part_keys[5], (SHOTS,), 0, NX * NY), jax.random.fold_in(part_keys[5], 1), 0, (NX * NY) - 1).astype(jnp.int32)
    wavelet = noise(part_keys[6], (STEPS, SHOTS), 3.0, 12.0, ((1, 4),), jnp.float32)
    receiver_cell = with_ends(jax.random.randint(part_keys[7], (SHOTS, RECV), 0, NX * NY), jax.random.fold_in(part_keys[7], 1), 0, (NX * NY) - 1).astype(jnp.int32)
    traces = noise(part_keys[8], (STEPS, SHOTS, RECV), 2.0, 10.0, ((1, 4),), jnp.float32)
    offset_perm = jax.random.permutation(part_keys[9], OFFSETS).astype(jnp.int32)
    return {"source_now": source_now, "source_prev": source_prev, "receiver_now": receiver_now, "receiver_prev": receiver_prev, "courant_sq": courant_sq, "source_cell": source_cell, "wavelet": wavelet, "receiver_cell": receiver_cell, "traces": traces, "offset_perm": offset_perm}


stencil_weights = (-205.0 / 72.0, 8.0 / 5.0, -1.0 / 5.0, 8.0 / 315.0, -1.0 / 560.0)
side_weight = 1.0 / 16.0


def laplace(wavefield):
    size_x, size_y, size_z = wavefield.shape[-3:]
    leading = [(0, 0)] * (wavefield.ndim - 3)
    padded = jnp.pad(wavefield, leading + [(4, 4)] * 3)
    summed = (1.0 + 2.0 * side_weight) * stencil_weights[0] * wavefield
    for distance in range(1, 5):
        weight = stencil_weights[distance]
        summed = summed + weight * (padded[..., 4 + distance:4 + distance + size_x, 4:4 + size_y, 4:4 + size_z] + padded[..., 4 - distance:4 - distance + size_x, 4:4 + size_y, 4:4 + size_z])
        summed = summed + side_weight * weight * (padded[..., 4:4 + size_x, 4 + distance:4 + distance + size_y, 4:4 + size_z] + padded[..., 4:4 + size_x, 4 - distance:4 - distance + size_y, 4:4 + size_z])
        summed = summed + side_weight * weight * (padded[..., 4:4 + size_x, 4:4 + size_y, 4 + distance:4 + distance + size_z] + padded[..., 4:4 + size_x, 4:4 + size_y, 4 - distance:4 - distance + size_z])
    return summed


def reference(source_now, source_prev, receiver_now, receiver_prev, courant_sq, source_cell, wavelet, receiver_cell, traces, offset_perm):
    fields = jnp.stack([source_now, receiver_now])
    before = jnp.stack([source_prev, receiver_prev])
    shot_index = jnp.arange(SHOTS, dtype=jnp.int32)
    shot_grid = jnp.broadcast_to(shot_index[:, None], receiver_cell.shape)
    for moment in range(STEPS):
        source_plane = jnp.zeros((SHOTS, NX * NY), jnp.float32).at[shot_index, source_cell].add(wavelet[moment])
        receiver_plane = jnp.zeros((SHOTS, NX * NY), jnp.float32).at[shot_grid, receiver_cell].add(traces[moment])
        planes = jnp.stack([source_plane, receiver_plane]).reshape(2, SHOTS, NX, NY)
        updated = 2.0 * fields - before + courant_sq * laplace(fields)
        updated = updated.at[:, :, :, :, INJECT_Z].add(planes)
        before, fields = fields, updated
    half_span = OFFSETS // 2
    source_pad = jnp.pad(fields[0], ((0, 0), (0, 0), (half_span, half_span), (0, 0)))
    receiver_pad = jnp.pad(fields[1], ((0, 0), (0, 0), (half_span, half_span), (0, 0)))

    def one_offset(lag_index):
        shift_by = lag_index - half_span
        shifted_source = lax.dynamic_slice_in_dim(source_pad, half_span - shift_by, NY, axis=2)
        shifted_receiver = lax.dynamic_slice_in_dim(receiver_pad, half_span + shift_by, NY, axis=2)
        return jnp.sum(shifted_source * shifted_receiver, axis=0)

    offset_image = lax.map(one_offset, offset_perm)
    return offset_image, fields[0], fields[1]
```

```python
import functools

import jax
import jax.numpy as jnp
from jax import lax
from jax.experimental import pallas as pl
from jax.experimental.pallas import tpu as pltpu
from jax.sharding import PartitionSpec as P

STEPS = 8
INJECT_Z = 4
REACH = 4
CHUNK = 4
LANES = 128
MESH = pl.DeviceIdType.MESH

stencil_weights = (-205.0 / 72.0, 8.0 / 5.0, -1.0 / 5.0, 8.0 / 315.0, -1.0 / 560.0)
side_weight = 1.0 / 16.0


def split_two(values):
    high = values.astype(jnp.bfloat16)
    low = (values - high.astype(jnp.float32)).astype(jnp.bfloat16)
    return high, low


def band(size, block):
    i = lax.broadcasted_iota(jnp.int32, (size, size), 0)
    j = lax.broadcasted_iota(jnp.int32, (size, size), 1)
    gap = jnp.abs(i - j)
    out = jnp.zeros((size, size), jnp.float32)
    for distance in range(1, REACH + 1):
        out = jnp.where(gap == distance, side_weight * stencil_weights[distance], out)
    if block < size:
        out = jnp.where(i // block == j // block, out, 0.0)
    return out


def dot(a, b):
    return jnp.dot(a, b, preferred_element_type=jnp.float32)


def kernel(
    source_now, source_prev, receiver_now, receiver_prev, courant, source_cell, wavelet,
    receiver_cell, traces, perm, image_out, source_out, receiver_out,
    buf, cbuf, mbuf, inject, trace_rows, z_hi, z_lo, y_hi, y_lo,
    part, send_a, recv_a, send_b, recv_b, image,
    load_sem, halo_send, halo_recv, a_send, a_recv, b_send, b_recv, out_sem,
):
    shots, rows, ny, nz = source_now.shape
    fields = 2 * shots
    cells = rows * ny
    offsets = perm.shape[0]
    half = offsets // 2
    slabs = lax.axis_size("slab")
    shot_devices = lax.axis_size("shot")
    per_device = offsets // shot_devices
    slab = lax.axis_index("slab")
    me = lax.axis_index("shot")
    has_low = slab > 0
    has_high = slab < slabs - 1
    near = me + 1 - 2 * (me % 2)
    far = (me + shot_devices // 2) % shot_devices
    near_far = (near + shot_devices // 2) % shot_devices

    barrier = pltpu.get_barrier_semaphore()

    @pl.when(has_low)
    def _():
        pl.semaphore_signal(barrier, inc=1, device_id={"slab": slab - 1}, device_id_type=MESH)

    @pl.when(has_high)
    def _():
        pl.semaphore_signal(barrier, inc=1, device_id={"slab": slab + 1}, device_id_type=MESH)

    pl.semaphore_signal(barrier, inc=1, device_id={"shot": near}, device_id_type=MESH)
    pl.semaphore_signal(barrier, inc=1, device_id={"shot": far}, device_id_type=MESH)

    body_rows = pl.ds(REACH, rows)
    loads = []
    for w in range(fields):
        now, before = ((source_now, source_prev), (receiver_now, receiver_prev))[w % 2]
        loads.append(pltpu.make_async_copy(now.at[w // 2], buf.at[0, w, body_rows], load_sem.at[2 * w]))
        loads.append(pltpu.make_async_copy(before.at[w // 2], buf.at[1, w, body_rows], load_sem.at[2 * w + 1]))
    loads.append(pltpu.make_async_copy(courant, cbuf, load_sem.at[2 * fields]))
    for load in loads:
        load.start()

    pl.semaphore_wait(barrier, 2 + has_low.astype(jnp.int32) + has_high.astype(jnp.int32))

    def to_low(source, p, w):
        return pltpu.make_async_remote_copy(
            src_ref=source, dst_ref=buf.at[p, w, pl.ds(REACH + rows, REACH)],
            send_sem=halo_send.at[w, 0], recv_sem=halo_recv.at[p, w, 1],
            device_id={"slab": slab - 1}, device_id_type=MESH)

    def to_high(source, p, w):
        return pltpu.make_async_remote_copy(
            src_ref=source, dst_ref=buf.at[p, w, pl.ds(0, REACH)],
            send_sem=halo_send.at[w, 1], recv_sem=halo_recv.at[p, w, 0],
            device_id={"slab": slab + 1}, device_id_type=MESH)

    def low_rows(p, w):
        return buf.at[p, w, pl.ds(REACH, REACH)]

    def high_rows(p, w):
        return buf.at[p, w, pl.ds(rows, REACH)]

    for w in range(fields):
        now = (source_now, receiver_now)[w % 2]

        @pl.when(has_low)
        def _():
            to_low(now.at[w // 2, pl.ds(0, REACH)], 0, w).start()

        @pl.when(has_high)
        def _():
            to_high(now.at[w // 2, pl.ds(rows - REACH, REACH)], 0, w).start()

    edge = jnp.zeros((REACH, ny, nz), jnp.float32)

    @pl.when(slab == 0)
    def _():
        for w in range(fields):
            for p in range(2):
                buf[p, w, 0:REACH] = edge

    @pl.when(slab == slabs - 1)
    def _():
        for w in range(fields):
            for p in range(2):
                buf[p, w, REACH + rows : 2 * REACH + rows] = edge

    z_hi[...], z_lo[...] = split_two(band(nz, nz))
    y_hi[...], y_lo[...] = split_two(band(cells, ny))

    first = slab * cells
    lane = lax.broadcasted_iota(jnp.int32, (1, LANES), 1)
    cell_lanes = lax.broadcasted_iota(jnp.int32, (cells, LANES), 0) + first
    trace_rows[...] = jnp.zeros(trace_rows.shape, jnp.float32)
    for s in range(shots):
        amplitude = jnp.zeros((1, LANES), jnp.float32)
        for t in range(STEPS):
            amplitude = jnp.where(lane == (INJECT_Z - t) % LANES, wavelet[t, s], amplitude)
        inject[2 * s] = jnp.where(cell_lanes == source_cell[s], amplitude, 0.0)
        receivers = receiver_cell.shape[1]
        positions = lax.broadcasted_iota(jnp.int32, (cells, receivers), 0) + first
        hot = jnp.where(positions == receiver_cell[pl.ds(s, 1), :], 1.0, 0.0).astype(jnp.bfloat16)
        for t in range(STEPS):
            trace_rows[pl.ds((INJECT_Z - t) % LANES, 1), :] = traces[t, pl.ds(s, 1), :]
        amounts = trace_rows[...]
        high, rest = split_two(amounts)
        left = amounts - high.astype(jnp.float32)
        rest, low = split_two(left)
        total = jnp.zeros((cells, LANES), jnp.float32)
        for piece in (low, rest, high):
            total = total + lax.dot_general(
                hot, piece, (((1,), (1,)), ((), ())), preferred_element_type=jnp.float32)
        inject[2 * s + 1] = total

    for load in loads:
        load.wait()

    at_depth = lax.broadcasted_iota(jnp.int32, (CHUNK, ny, LANES), 2) == INJECT_Z

    def side_terms(p, w):
        values = buf[p, w, REACH : REACH + rows].reshape(cells, nz)
        high, low = split_two(values)
        total = dot(low, z_hi[...]) + dot(high, z_lo[...]) + dot(high, z_hi[...])
        total = total + (dot(y_hi[...], low) + dot(y_lo[...], high) + dot(y_hi[...], high))
        mbuf[w] = total.reshape(rows, ny, nz)

    def advance(p, q, w, r):
        centre = buf[p, w, REACH + r : REACH + r + CHUNK]
        total = (1.0 + 2.0 * side_weight) * stencil_weights[0] * centre + mbuf[w, r : r + CHUNK]
        for k in range(1, REACH + 1):
            total = total + stencil_weights[k] * (
                buf[p, w, REACH + r + k : REACH + r + k + CHUNK]
                + buf[p, w, REACH + r - k : REACH + r - k + CHUNK])
        updated = 2.0 * centre - buf[q, w, REACH + r : REACH + r + CHUNK] + cbuf[r : r + CHUNK] * total
        here = pl.ds(r * ny, CHUNK * ny)
        plane = inject[w, here, :]
        added = jnp.where(at_depth, plane.reshape(CHUNK, ny, LANES), 0.0)
        buf[q, w, REACH + r : REACH + r + CHUNK, :, 0:LANES] = updated[:, :, 0:LANES] + added
        if nz > LANES:
            buf[q, w, REACH + r : REACH + r + CHUNK, :, LANES:nz] = updated[:, :, LANES:nz]
        inject[w, here, :] = pltpu.roll(plane, 1, 1)

    def wait_low(p, w):
        @pl.when(has_low)
        def _():
            to_high(high_rows(p, w), p, w).wait_recv()
            to_low(low_rows(p, w), p, w).wait_send()

    def wait_high(p, w):
        @pl.when(has_high)
        def _():
            to_low(low_rows(p, w), p, w).wait_recv()
            to_high(high_rows(p, w), p, w).wait_send()

    def step(t, carry):
        p = t % 2
        q = 1 - p
        for w in range(fields):
            side_terms(p, w)
            for r in range(REACH, rows - REACH, CHUNK):
                advance(p, q, w, r)
            wait_low(p, w)
            advance(p, q, w, 0)

            @pl.when(has_low)
            def _():
                to_low(low_rows(q, w), q, w).start()

            wait_high(p, w)
            advance(p, q, w, rows - CHUNK)

            @pl.when(has_high)
            def _():
                to_high(high_rows(q, w), q, w).start()
        return carry

    lax.fori_loop(0, STEPS - 1, step, 0)

    p = (STEPS - 1) % 2
    q = 1 - p
    y_index = lax.broadcasted_iota(jnp.int32, (CHUNK, ny, nz), 1)

    def copy_a(group, b):
        block = pl.ds(b * CHUNK, CHUNK)
        return pltpu.make_async_remote_copy(
            src_ref=send_a.at[group, :, block], dst_ref=recv_a.at[group, :, block],
            send_sem=a_send.at[group, b], recv_sem=a_recv.at[group, b],
            device_id={"shot": near}, device_id_type=MESH)

    def copy_b(b):
        block = pl.ds(b * CHUNK, CHUNK)
        return pltpu.make_async_remote_copy(
            src_ref=send_b.at[:, block], dst_ref=recv_b.at[:, block],
            send_sem=b_send.at[b], recv_sem=b_recv.at[b],
            device_id={"shot": far}, device_id_type=MESH)

    def correlate(b):
        r = b * CHUNK
        block = slice(REACH + r, REACH + r + CHUNK)
        for k in range(offsets):
            h = k - half
            total = None
            for s in range(shots):
                source = buf[q, 2 * s, block]
                receiver = buf[q, 2 * s + 1, block]
                if h % ny:
                    source = pltpu.roll(source, h % ny, 1)
                    receiver = pltpu.roll(receiver, (-h) % ny, 1)
                total = source * receiver if total is None else total + source * receiver
            if h:
                total = jnp.where((y_index >= abs(h)) & (y_index < ny - abs(h)), total, 0.0)
            part[k, r : r + CHUNK] = total
        for group, device in ((0, near_far), (1, near)):
            for j in range(per_device):
                send_a[group, j, r : r + CHUNK] = part[perm[device * per_device + j], r : r + CHUNK]
            copy_a(group, b).start()

    def relay(b):
        r = b * CHUNK
        copy_a(0, b).wait_recv()
        for j in range(per_device):
            send_b[j, r : r + CHUNK] = (
                part[perm[far * per_device + j], r : r + CHUNK] + recv_a[0, j, r : r + CHUNK])
        copy_b(b).start()

    def finish(b):
        r = b * CHUNK
        copy_a(1, b).wait_recv()
        copy_b(b).wait_recv()
        for j in range(per_device):
            image[j, r : r + CHUNK] = (
                part[perm[me * per_device + j], r : r + CHUNK]
                + recv_a[1, j, r : r + CHUNK] + recv_b[j, r : r + CHUNK])
        block = pl.ds(r, CHUNK)
        pltpu.make_async_copy(image.at[:, block], image_out.at[:, block], out_sem.at[b]).start()

    blocks = rows // CHUNK
    inner = list(range(1, blocks - 1))
    outer = [0, blocks - 1]
    for w in range(fields):
        side_terms(p, w)
        for b in inner:
            advance(p, q, w, b * CHUNK)
    for b in inner:
        correlate(b)
    for b in inner:
        relay(b)
    stores = []
    for w in range(fields):
        wait_low(p, w)
        advance(p, q, w, 0)
        wait_high(p, w)
        advance(p, q, w, rows - CHUNK)
        out = (source_out, receiver_out)[w % 2]
        stores.append(pltpu.make_async_copy(buf.at[q, w, body_rows], out.at[w // 2], out_sem.at[blocks + w]))
        stores[-1].start()
    for b in outer:
        correlate(b)
    for b in outer:
        relay(b)
    for b in inner + outer:
        finish(b)
    for b in range(blocks):
        copy_a(0, b).wait_send()
        copy_a(1, b).wait_send()
        copy_b(b).wait_send()
        block = pl.ds(b * CHUNK, CHUNK)
        pltpu.make_async_copy(image.at[:, block], image_out.at[:, block], out_sem.at[b]).wait()
    for store in stores:
        store.wait()


def body(
    source_now, source_prev, receiver_now, receiver_prev, courant_sq, source_cell, wavelet,
    receiver_cell, traces, offset_perm,
):
    shots, rows, ny, nz = source_now.shape
    fields = 2 * shots
    cells = rows * ny
    offsets = offset_perm.shape[0]
    per_device = offsets // lax.axis_size("shot")
    blocks = rows // CHUNK
    anywhere = pl.BlockSpec(memory_space=pl.ANY)
    vector = pl.BlockSpec(memory_space=pltpu.VMEM)
    scalar = pl.BlockSpec(memory_space=pltpu.SMEM)
    f32 = jnp.float32
    field = jax.ShapeDtypeStruct(source_now.shape, f32)
    images = jax.ShapeDtypeStruct((per_device, rows, ny, nz), f32)
    return pl.pallas_call(
        kernel,
        out_shape=(images, field, field),
        in_specs=[anywhere] * 5 + [scalar, scalar, vector, vector, scalar],
        out_specs=(anywhere,) * 3,
        scratch_shapes=[
            pltpu.VMEM((2, fields, rows + 2 * REACH, ny, nz), f32),
            pltpu.VMEM((rows, ny, nz), f32),
            pltpu.VMEM((fields, rows, ny, nz), f32),
            pltpu.VMEM((fields, cells, LANES), f32),
            pltpu.VMEM((LANES, receiver_cell.shape[1]), f32),
            pltpu.VMEM((nz, nz), jnp.bfloat16),
            pltpu.VMEM((nz, nz), jnp.bfloat16),
            pltpu.VMEM((cells, cells), jnp.bfloat16),
            pltpu.VMEM((cells, cells), jnp.bfloat16),
            pltpu.VMEM((offsets, rows, ny, nz), f32),
            pltpu.VMEM((2, per_device, rows, ny, nz), f32),
            pltpu.VMEM((2, per_device, rows, ny, nz), f32),
            pltpu.VMEM((per_device, rows, ny, nz), f32),
            pltpu.VMEM((per_device, rows, ny, nz), f32),
            pltpu.VMEM((per_device, rows, ny, nz), f32),
            pltpu.SemaphoreType.DMA((2 * fields + 1,)),
            pltpu.SemaphoreType.DMA((fields, 2)),
            pltpu.SemaphoreType.DMA((2, fields, 2)),
            pltpu.SemaphoreType.DMA((2, blocks)),
            pltpu.SemaphoreType.DMA((2, blocks)),
            pltpu.SemaphoreType.DMA((blocks,)),
            pltpu.SemaphoreType.DMA((blocks,)),
            pltpu.SemaphoreType.DMA((blocks + fields,)),
        ],
        compiler_params=pltpu.CompilerParams(
            collective_id=0, has_side_effects=True, vmem_limit_bytes=40 * 1024 * 1024
        ),
    )(
        source_now, source_prev, receiver_now, receiver_prev, courant_sq, source_cell, wavelet,
        receiver_cell, traces, offset_perm,
    )


def solution(mesh):
    field = P(("runs", "shot"), "slab", None, None)
    in_specs = (
        field, field, field, field,
        P(("runs", "slab"), None, None),
        P(("runs", "shot")),
        P(None, ("runs", "shot")),
        P(("runs", "shot"), None),
        P(None, ("runs", "shot"), None),
        P("runs"),
    )
    return jax.shard_map(body, mesh=mesh, in_specs=in_specs, out_specs=(field,) * 3, check_vma=False)
```

```python
import functools

import jax
import jax.numpy as jnp
from jax import lax
from jax.experimental import pallas as pl
from jax.experimental.pallas import tpu as pltpu
from jax.sharding import PartitionSpec as P

STEPS = 8
INJECT_Z = 4
REACH = 4
CHUNK = 4
LANES = 128
GRANT = 62 * 1024 * 1024
MESH = pl.DeviceIdType.MESH

stencil_weights = (-205.0 / 72.0, 8.0 / 5.0, -1.0 / 5.0, 8.0 / 315.0, -1.0 / 560.0)
side_weight = 1.0 / 16.0


def split_two(values):
    high = values.astype(jnp.bfloat16)
    low = (values - high.astype(jnp.float32)).astype(jnp.bfloat16)
    return high, low


def band(size, block):
    i = lax.broadcasted_iota(jnp.int32, (size, size), 0)
    j = lax.broadcasted_iota(jnp.int32, (size, size), 1)
    gap = jnp.abs(i - j)
    out = jnp.zeros((size, size), jnp.float32)
    for distance in range(1, REACH + 1):
        out = jnp.where(gap == distance, side_weight * stencil_weights[distance], out)
    if block < size:
        out = jnp.where(i // block == j // block, out, 0.0)
    return out


def dot(a, b):
    return jnp.dot(a, b, preferred_element_type=jnp.float32)


def kernel(
    source_now, source_prev, receiver_now, receiver_prev, courant, source_cell, wavelet,
    receiver_cell, traces_far, perm, image_out, source_out, receiver_out,
    buf, cbuf, mbuf, inject, trace_rows, z_hi, z_lo, y_hi, y_lo,
    part, send_a, recv_a, send_b, recv_b, image, traces,
    load_sem, halo_send, halo_recv, a_send, a_recv, b_send, b_recv, out_sem,
):
    shots, rows, ny, nz = source_now.shape
    fields = 2 * shots
    cells = rows * ny
    offsets = perm.shape[0]
    half = offsets // 2
    slabs = lax.axis_size("slab")
    shot_devices = lax.axis_size("shot")
    per_device = offsets // shot_devices
    slab = lax.axis_index("slab")
    me = lax.axis_index("shot")
    has_low = slab > 0
    has_high = slab < slabs - 1
    near = me + 1 - 2 * (me % 2)
    far = (me + shot_devices // 2) % shot_devices
    near_far = (near + shot_devices // 2) % shot_devices

    barrier = pltpu.get_barrier_semaphore()

    @pl.when(has_low)
    def _():
        pl.semaphore_signal(barrier, inc=1, device_id={"slab": slab - 1}, device_id_type=MESH)

    @pl.when(has_high)
    def _():
        pl.semaphore_signal(barrier, inc=1, device_id={"slab": slab + 1}, device_id_type=MESH)

    pl.semaphore_signal(barrier, inc=1, device_id={"shot": near}, device_id_type=MESH)
    pl.semaphore_signal(barrier, inc=1, device_id={"shot": far}, device_id_type=MESH)

    body_rows = pl.ds(REACH, rows)
    loads = []
    for w in range(fields):
        now, before = ((source_now, source_prev), (receiver_now, receiver_prev))[w % 2]
        loads.append(pltpu.make_async_copy(now.at[w // 2], buf.at[0, w, body_rows], load_sem.at[2 * w]))
        loads.append(pltpu.make_async_copy(before.at[w // 2], buf.at[1, w, body_rows], load_sem.at[2 * w + 1]))
    loads.append(pltpu.make_async_copy(courant, cbuf, load_sem.at[2 * fields]))
    trace_load = pltpu.make_async_copy(traces_far, traces, load_sem.at[2 * fields + 1])
    trace_load.start()
    for load in loads:
        load.start()

    pl.semaphore_wait(barrier, 2 + has_low.astype(jnp.int32) + has_high.astype(jnp.int32))

    def to_low(source, p, w):
        return pltpu.make_async_remote_copy(
            src_ref=source, dst_ref=buf.at[p, w, pl.ds(REACH + rows, REACH)],
            send_sem=halo_send.at[w, 0], recv_sem=halo_recv.at[p, w, 1],
            device_id={"slab": slab - 1}, device_id_type=MESH)

    def to_high(source, p, w):
        return pltpu.make_async_remote_copy(
            src_ref=source, dst_ref=buf.at[p, w, pl.ds(0, REACH)],
            send_sem=halo_send.at[w, 1], recv_sem=halo_recv.at[p, w, 0],
            device_id={"slab": slab + 1}, device_id_type=MESH)

    def low_rows(p, w):
        return buf.at[p, w, pl.ds(REACH, REACH)]

    def high_rows(p, w):
        return buf.at[p, w, pl.ds(rows, REACH)]

    for w in range(fields):
        now = (source_now, receiver_now)[w % 2]

        @pl.when(has_low)
        def _():
            to_low(now.at[w // 2, pl.ds(0, REACH)], 0, w).start()

        @pl.when(has_high)
        def _():
            to_high(now.at[w // 2, pl.ds(rows - REACH, REACH)], 0, w).start()

    edge = jnp.zeros((REACH, ny, nz), jnp.float32)

    @pl.when(slab == 0)
    def _():
        for w in range(fields):
            for p in range(2):
                buf[p, w, 0:REACH] = edge

    @pl.when(slab == slabs - 1)
    def _():
        for w in range(fields):
            for p in range(2):
                buf[p, w, REACH + rows : 2 * REACH + rows] = edge

    z_hi[...], z_lo[...] = split_two(band(nz, nz))
    y_hi[...], y_lo[...] = split_two(band(cells, ny))

    first = slab * cells
    lane = lax.broadcasted_iota(jnp.int32, (1, LANES), 1)
    cell_lanes = lax.broadcasted_iota(jnp.int32, (cells, LANES), 0) + first
    trace_rows[...] = jnp.zeros(trace_rows.shape, jnp.float32)
    trace_load.wait()
    for s in range(shots):
        amplitude = jnp.zeros((1, LANES), jnp.float32)
        for t in range(STEPS):
            amplitude = jnp.where(lane == (INJECT_Z - t) % LANES, wavelet[s, t], amplitude)
        inject[2 * s] = jnp.where(cell_lanes == source_cell[s], amplitude, 0.0)
        receivers = receiver_cell.shape[1]
        positions = lax.broadcasted_iota(jnp.int32, (cells, receivers), 0) + first
        hot = jnp.where(positions == receiver_cell[pl.ds(s, 1), :], 1.0, 0.0).astype(jnp.bfloat16)
        for t in range(STEPS):
            trace_rows[pl.ds((INJECT_Z - t) % LANES, 1), :] = traces[t, pl.ds(s, 1), :]
        amounts = trace_rows[...]
        high, rest = split_two(amounts)
        left = amounts - high.astype(jnp.float32)
        rest, low = split_two(left)
        total = jnp.zeros((cells, LANES), jnp.float32)
        for piece in (low, rest, high):
            total = total + lax.dot_general(
                hot, piece, (((1,), (1,)), ((), ())), preferred_element_type=jnp.float32)
        inject[2 * s + 1] = total

    for load in loads:
        load.wait()

    at_depth = lax.broadcasted_iota(jnp.int32, (CHUNK, ny, LANES), 2) == INJECT_Z

    def side_terms(p, w):
        values = buf[p, w, REACH : REACH + rows].reshape(cells, nz)
        high, low = split_two(values)
        total = dot(low, z_hi[...]) + dot(high, z_lo[...]) + dot(high, z_hi[...])
        total = total + (dot(y_hi[...], low) + dot(y_lo[...], high) + dot(y_hi[...], high))
        mbuf[w] = total.reshape(rows, ny, nz)

    def advance(p, q, w, r):
        centre = buf[p, w, REACH + r : REACH + r + CHUNK]
        total = (1.0 + 2.0 * side_weight) * stencil_weights[0] * centre + mbuf[w, r : r + CHUNK]
        for k in range(1, REACH + 1):
            total = total + stencil_weights[k] * (
                buf[p, w, REACH + r + k : REACH + r + k + CHUNK]
                + buf[p, w, REACH + r - k : REACH + r - k + CHUNK])
        updated = 2.0 * centre - buf[q, w, REACH + r : REACH + r + CHUNK] + cbuf[r : r + CHUNK] * total
        here = pl.ds(r * ny, CHUNK * ny)
        plane = inject[w, here, :]
        added = jnp.where(at_depth, plane.reshape(CHUNK, ny, LANES), 0.0)
        buf[q, w, REACH + r : REACH + r + CHUNK, :, 0:LANES] = updated[:, :, 0:LANES] + added
        if nz > LANES:
            buf[q, w, REACH + r : REACH + r + CHUNK, :, LANES:nz] = updated[:, :, LANES:nz]
        inject[w, here, :] = pltpu.roll(plane, 1, 1)

    def wait_low(p, w):
        @pl.when(has_low)
        def _():
            to_high(high_rows(p, w), p, w).wait_recv()
            to_low(low_rows(p, w), p, w).wait_send()

    def wait_high(p, w):
        @pl.when(has_high)
        def _():
            to_low(low_rows(p, w), p, w).wait_recv()
            to_high(high_rows(p, w), p, w).wait_send()

    def step(t, carry):
        p = t % 2
        q = 1 - p
        for w in range(fields):
            side_terms(p, w)
            for r in range(REACH, rows - REACH, CHUNK):
                advance(p, q, w, r)
            wait_low(p, w)
            advance(p, q, w, 0)

            @pl.when(has_low)
            def _():
                to_low(low_rows(q, w), q, w).start()

            wait_high(p, w)
            advance(p, q, w, rows - CHUNK)

            @pl.when(has_high)
            def _():
                to_high(high_rows(q, w), q, w).start()
        return carry

    lax.fori_loop(0, STEPS - 1, step, 0)

    p = (STEPS - 1) % 2
    q = 1 - p
    y_index = lax.broadcasted_iota(jnp.int32, (CHUNK, ny, nz), 1)

    def copy_a(group, b):
        block = pl.ds(b * CHUNK, CHUNK)
        return pltpu.make_async_remote_copy(
            src_ref=send_a.at[group, :, block], dst_ref=recv_a.at[group, :, block],
            send_sem=a_send.at[group, b], recv_sem=a_recv.at[group, b],
            device_id={"shot": near}, device_id_type=MESH)

    def copy_b(b):
        block = pl.ds(b * CHUNK, CHUNK)
        return pltpu.make_async_remote_copy(
            src_ref=send_b.at[:, block], dst_ref=recv_b.at[:, block],
            send_sem=b_send.at[b], recv_sem=b_recv.at[b],
            device_id={"shot": far}, device_id_type=MESH)

    def correlate(b):
        r = b * CHUNK
        block = slice(REACH + r, REACH + r + CHUNK)
        for k in range(offsets):
            h = k - half
            total = None
            for s in range(shots):
                source = buf[q, 2 * s, block]
                receiver = buf[q, 2 * s + 1, block]
                if h % ny:
                    source = pltpu.roll(source, h % ny, 1)
                    receiver = pltpu.roll(receiver, (-h) % ny, 1)
                total = source * receiver if total is None else total + source * receiver
            if h:
                total = jnp.where((y_index >= abs(h)) & (y_index < ny - abs(h)), total, 0.0)
            part[k, r : r + CHUNK] = total
        for group, device in ((0, near_far), (1, near)):
            for j in range(per_device):
                send_a[group, j, r : r + CHUNK] = part[perm[device * per_device + j], r : r + CHUNK]
            copy_a(group, b).start()

    def relay(b):
        r = b * CHUNK
        copy_a(0, b).wait_recv()
        for j in range(per_device):
            send_b[j, r : r + CHUNK] = (
                part[perm[far * per_device + j], r : r + CHUNK] + recv_a[0, j, r : r + CHUNK])
        copy_b(b).start()

    def finish(b):
        r = b * CHUNK
        copy_a(1, b).wait_recv()
        copy_b(b).wait_recv()
        for j in range(per_device):
            image[j, r : r + CHUNK] = (
                part[perm[me * per_device + j], r : r + CHUNK]
                + recv_a[1, j, r : r + CHUNK] + recv_b[j, r : r + CHUNK])
        block = pl.ds(r, CHUNK)
        pltpu.make_async_copy(image.at[:, block], image_out.at[:, block], out_sem.at[b]).start()

    blocks = rows // CHUNK
    inner = list(range(1, blocks - 1))
    outer = [0, blocks - 1]
    for w in range(fields):
        side_terms(p, w)
        for b in inner:
            advance(p, q, w, b * CHUNK)
    for b in inner:
        correlate(b)
    for b in inner:
        relay(b)
    stores = []
    for w in range(fields):
        wait_low(p, w)
        advance(p, q, w, 0)
        wait_high(p, w)
        advance(p, q, w, rows - CHUNK)
        out = (source_out, receiver_out)[w % 2]
        stores.append(pltpu.make_async_copy(buf.at[q, w, body_rows], out.at[w // 2], out_sem.at[blocks + w]))
        stores[-1].start()
    for b in outer:
        correlate(b)
    for b in outer:
        relay(b)
    for b in inner + outer:
        finish(b)
    for b in range(blocks):
        copy_a(0, b).wait_send()
        copy_a(1, b).wait_send()
        copy_b(b).wait_send()
        block = pl.ds(b * CHUNK, CHUNK)
        pltpu.make_async_copy(image.at[:, block], image_out.at[:, block], out_sem.at[b]).wait()
    for store in stores:
        store.wait()


def store_kernel(image, source, receiver, image_out, source_out, receiver_out, sem):
    pairs = ((image, image_out), (source, source_out), (receiver, receiver_out))
    copies = [
        pltpu.make_async_copy(a.at[j], b.at[j], sem.at[i, j])
        for i, (a, b) in enumerate(pairs) for j in range(a.shape[0])
    ]
    for copy in copies:
        copy.start()
    for copy in copies:
        copy.wait()


def body(
    source_now, source_prev, receiver_now, receiver_prev, courant_sq, source_cell, wavelet,
    receiver_cell, traces, offset_perm,
):
    shots, rows, ny, nz = source_now.shape
    fields = 2 * shots
    cells = rows * ny
    offsets = offset_perm.shape[0]
    per_device = offsets // lax.axis_size("shot")
    blocks = rows // CHUNK
    anywhere = pl.BlockSpec(memory_space=pl.ANY)
    main = pl.BlockSpec(memory_space=pltpu.HBM)
    vector = pl.BlockSpec(memory_space=pltpu.VMEM)
    scalar = pl.BlockSpec(memory_space=pltpu.SMEM)
    f32 = jnp.float32
    field = jax.ShapeDtypeStruct(source_now.shape, f32)
    images = jax.ShapeDtypeStruct((per_device, rows, ny, nz), f32)
    results = pl.pallas_call(
        kernel,
        out_shape=(images, field, field),
        in_specs=[main] * 5 + [scalar, scalar, vector, main, scalar],
        out_specs=(anywhere,) * 3,
        scratch_shapes=[
            pltpu.VMEM((2, fields, rows + 2 * REACH, ny, nz), f32),
            pltpu.VMEM((rows, ny, nz), f32),
            pltpu.VMEM((fields, rows, ny, nz), f32),
            pltpu.VMEM((fields, cells, LANES), f32),
            pltpu.VMEM((LANES, receiver_cell.shape[1]), f32),
            pltpu.VMEM((nz, nz), jnp.bfloat16),
            pltpu.VMEM((nz, nz), jnp.bfloat16),
            pltpu.VMEM((cells, cells), jnp.bfloat16),
            pltpu.VMEM((cells, cells), jnp.bfloat16),
            pltpu.VMEM((offsets, rows, ny, nz), f32),
            pltpu.VMEM((2, per_device, rows, ny, nz), f32),
            pltpu.VMEM((2, per_device, rows, ny, nz), f32),
            pltpu.VMEM((per_device, rows, ny, nz), f32),
            pltpu.VMEM((per_device, rows, ny, nz), f32),
            pltpu.VMEM((per_device, rows, ny, nz), f32),
            pltpu.VMEM(traces.shape, f32),
            pltpu.SemaphoreType.DMA((2 * fields + 2,)),
            pltpu.SemaphoreType.DMA((fields, 2)),
            pltpu.SemaphoreType.DMA((2, fields, 2)),
            pltpu.SemaphoreType.DMA((2, blocks)),
            pltpu.SemaphoreType.DMA((2, blocks)),
            pltpu.SemaphoreType.DMA((blocks,)),
            pltpu.SemaphoreType.DMA((blocks,)),
            pltpu.SemaphoreType.DMA((blocks + fields,)),
        ],
        compiler_params=pltpu.CompilerParams(
            collective_id=0, has_side_effects=True, vmem_limit_bytes=GRANT
        ),
    )(
        source_now, source_prev, receiver_now, receiver_prev, courant_sq, source_cell, wavelet.T,
        receiver_cell, traces, offset_perm,
    )
    return pl.pallas_call(
        store_kernel,
        out_shape=(images, field, field),
        in_specs=[anywhere] * 3,
        out_specs=(main,) * 3,
        scratch_shapes=[pltpu.SemaphoreType.DMA((3, max(shots, per_device)))],
        compiler_params=pltpu.CompilerParams(vmem_limit_bytes=GRANT),
    )(*results)


def solution(mesh):
    field = P(("runs", "shot"), "slab", None, None)
    in_specs = (
        field, field, field, field,
        P(("runs", "slab"), None, None),
        P(("runs", "shot")),
        P(None, ("runs", "shot")),
        P(("runs", "shot"), None),
        P(None, ("runs", "shot"), None),
        P("runs"),
    )
    return jax.shard_map(body, mesh=mesh, in_specs=in_specs, out_specs=(field,) * 3, check_vma=False)
```

```python
import functools

import jax
import jax.numpy as jnp
from jax import lax
from jax.experimental import pallas as pl
from jax.experimental.pallas import tpu as pltpu
from jax.sharding import PartitionSpec as P

STEPS = 8
INJECT_Z = 4
REACH = 4
CHUNK = 4
LANES = 128
GRANT = 62 * 1024 * 1024
MESH = pl.DeviceIdType.MESH

stencil_weights = (-205.0 / 72.0, 8.0 / 5.0, -1.0 / 5.0, 8.0 / 315.0, -1.0 / 560.0)
side_weight = 1.0 / 16.0


def split_two(values):
    high = values.astype(jnp.bfloat16)
    low = (values - high.astype(jnp.float32)).astype(jnp.bfloat16)
    return high, low


def band(size, block):
    i = lax.broadcasted_iota(jnp.int32, (size, size), 0)
    j = lax.broadcasted_iota(jnp.int32, (size, size), 1)
    gap = jnp.abs(i - j)
    out = jnp.zeros((size, size), jnp.float32)
    for distance in range(1, REACH + 1):
        out = jnp.where(gap == distance, side_weight * stencil_weights[distance], out)
    if block < size:
        out = jnp.where(i // block == j // block, out, 0.0)
    return out


def dot(a, b):
    return jnp.dot(a, b, preferred_element_type=jnp.float32)


def kernel(
    source_now, source_prev, receiver_now, receiver_prev, courant, source_cell, wavelet,
    receiver_cell, traces_far, perm, image_out, source_out, receiver_out,
    buf, cbuf, mbuf, inject, trace_rows, z_hi, z_lo, y_hi, y_lo,
    part, send_a, recv_a, send_b, recv_b, image, traces,
    load_sem, halo_send, halo_recv, a_send, a_recv, b_send, b_recv, out_sem,
):
    shots, rows, ny, nz = source_now.shape
    fields = 2 * shots
    cells = rows * ny
    offsets = perm.shape[0]
    half = offsets // 2
    slabs = lax.axis_size("slab")
    shot_devices = lax.axis_size("shot")
    per_device = offsets // shot_devices
    slab = lax.axis_index("slab")
    me = lax.axis_index("shot")
    has_low = slab > 0
    has_high = slab < slabs - 1
    near = me + 1 - 2 * (me % 2)
    far = (me + shot_devices // 2) % shot_devices
    near_far = (near + shot_devices // 2) % shot_devices

    barrier = pltpu.get_barrier_semaphore()

    @pl.when(has_low)
    def _():
        pl.semaphore_signal(barrier, inc=1, device_id={"slab": slab - 1}, device_id_type=MESH)

    @pl.when(has_high)
    def _():
        pl.semaphore_signal(barrier, inc=1, device_id={"slab": slab + 1}, device_id_type=MESH)

    pl.semaphore_signal(barrier, inc=1, device_id={"shot": near}, device_id_type=MESH)
    pl.semaphore_signal(barrier, inc=1, device_id={"shot": far}, device_id_type=MESH)

    body_rows = pl.ds(REACH, rows)
    loads = []
    for w in range(fields):
        now, before = ((source_now, source_prev), (receiver_now, receiver_prev))[w % 2]
        loads.append(pltpu.make_async_copy(now.at[w // 2], buf.at[0, w, body_rows], load_sem.at[2 * w]))
        loads.append(pltpu.make_async_copy(before.at[w // 2], buf.at[1, w, body_rows], load_sem.at[2 * w + 1]))
    loads.append(pltpu.make_async_copy(courant, cbuf, load_sem.at[2 * fields]))
    trace_load = pltpu.make_async_copy(traces_far, traces, load_sem.at[2 * fields + 1])
    trace_load.start()
    for load in loads:
        load.start()

    pl.semaphore_wait(barrier, 2 + has_low.astype(jnp.int32) + has_high.astype(jnp.int32))

    def to_low(source, p, w):
        return pltpu.make_async_remote_copy(
            src_ref=source, dst_ref=buf.at[p, w, pl.ds(REACH + rows, REACH)],
            send_sem=halo_send.at[w, 0], recv_sem=halo_recv.at[p, w, 1],
            device_id={"slab": slab - 1}, device_id_type=MESH)

    def to_high(source, p, w):
        return pltpu.make_async_remote_copy(
            src_ref=source, dst_ref=buf.at[p, w, pl.ds(0, REACH)],
            send_sem=halo_send.at[w, 1], recv_sem=halo_recv.at[p, w, 0],
            device_id={"slab": slab + 1}, device_id_type=MESH)

    def low_rows(p, w):
        return buf.at[p, w, pl.ds(REACH, REACH)]

    def high_rows(p, w):
        return buf.at[p, w, pl.ds(rows, REACH)]

    for w in range(fields):
        now = (source_now, receiver_now)[w % 2]

        @pl.when(has_low)
        def _():
            to_low(now.at[w // 2, pl.ds(0, REACH)], 0, w).start()

        @pl.when(has_high)
        def _():
            to_high(now.at[w // 2, pl.ds(rows - REACH, REACH)], 0, w).start()

    edge = jnp.zeros((REACH, ny, nz), jnp.float32)

    @pl.when(slab == 0)
    def _():
        for w in range(fields):
            for p in range(2):
                buf[p, w, 0:REACH] = edge

    @pl.when(slab == slabs - 1)
    def _():
        for w in range(fields):
            for p in range(2):
                buf[p, w, REACH + rows : 2 * REACH + rows] = edge

    z_hi[...], z_lo[...] = split_two(band(nz, nz))
    y_hi[...], y_lo[...] = split_two(band(cells, ny))

    first = slab * cells
    lane = lax.broadcasted_iota(jnp.int32, (1, LANES), 1)
    cell_lanes = lax.broadcasted_iota(jnp.int32, (cells, LANES), 0) + first
    trace_rows[...] = jnp.zeros(trace_rows.shape, jnp.float32)
    trace_load.wait()
    for s in range(shots):
        amplitude = jnp.zeros((1, LANES), jnp.float32)
        for t in range(STEPS):
            amplitude = jnp.where(lane == (INJECT_Z - t) % LANES, wavelet[s, t], amplitude)
        inject[2 * s] = jnp.where(cell_lanes == source_cell[s], amplitude, 0.0)
        receivers = receiver_cell.shape[1]
        positions = lax.broadcasted_iota(jnp.int32, (cells, receivers), 0) + first
        hot = jnp.where(positions == receiver_cell[pl.ds(s, 1), :], 1.0, 0.0).astype(jnp.bfloat16)
        for t in range(STEPS):
            trace_rows[pl.ds((INJECT_Z - t) % LANES, 1), :] = traces[t, pl.ds(s, 1), :]
        amounts = trace_rows[...]
        high, rest = split_two(amounts)
        left = amounts - high.astype(jnp.float32)
        rest, low = split_two(left)
        total = jnp.zeros((cells, LANES), jnp.float32)
        for piece in (low, rest, high):
            total = total + lax.dot_general(
                hot, piece, (((1,), (1,)), ((), ())), preferred_element_type=jnp.float32)
        inject[2 * s + 1] = total

    for load in loads:
        load.wait()

    at_depth = lax.broadcasted_iota(jnp.int32, (CHUNK, ny, LANES), 2) == INJECT_Z

    def side_terms(p, w):
        values = buf[p, w, REACH : REACH + rows].reshape(cells, nz)
        high, low = split_two(values)
        total = dot(low, z_hi[...]) + dot(high, z_lo[...]) + dot(high, z_hi[...])
        total = total + (dot(y_hi[...], low) + dot(y_lo[...], high) + dot(y_hi[...], high))
        mbuf[w] = total.reshape(rows, ny, nz)

    def advance(p, q, w, r):
        centre = buf[p, w, REACH + r : REACH + r + CHUNK]
        total = (1.0 + 2.0 * side_weight) * stencil_weights[0] * centre + mbuf[w, r : r + CHUNK]
        for k in range(1, REACH + 1):
            total = total + stencil_weights[k] * (
                buf[p, w, REACH + r + k : REACH + r + k + CHUNK]
                + buf[p, w, REACH + r - k : REACH + r - k + CHUNK])
        updated = 2.0 * centre - buf[q, w, REACH + r : REACH + r + CHUNK] + cbuf[r : r + CHUNK] * total
        here = pl.ds(r * ny, CHUNK * ny)
        plane = inject[w, here, :]
        added = jnp.where(at_depth, plane.reshape(CHUNK, ny, LANES), 0.0)
        buf[q, w, REACH + r : REACH + r + CHUNK, :, 0:LANES] = updated[:, :, 0:LANES] + added
        if nz > LANES:
            buf[q, w, REACH + r : REACH + r + CHUNK, :, LANES:nz] = updated[:, :, LANES:nz]
        inject[w, here, :] = pltpu.roll(plane, 1, 1)

    def wait_low(p, w):
        @pl.when(has_low)
        def _():
            to_high(high_rows(p, w), p, w).wait_recv()
            to_low(low_rows(p, w), p, w).wait_send()

    def wait_high(p, w):
        @pl.when(has_high)
        def _():
            to_low(low_rows(p, w), p, w).wait_recv()
            to_high(high_rows(p, w), p, w).wait_send()

    def step(t, carry):
        p = t % 2
        q = 1 - p
        for w in range(fields):
            side_terms(p, w)
            for r in range(REACH, rows - REACH, CHUNK):
                advance(p, q, w, r)
            wait_low(p, w)
            advance(p, q, w, 0)

            @pl.when(has_low)
            def _():
                to_low(low_rows(q, w), q, w).start()

            wait_high(p, w)
            advance(p, q, w, rows - CHUNK)

            @pl.when(has_high)
            def _():
                to_high(high_rows(q, w), q, w).start()
        return carry

    lax.fori_loop(0, STEPS - 1, step, 0)

    p = (STEPS - 1) % 2
    q = 1 - p
    y_index = lax.broadcasted_iota(jnp.int32, (CHUNK, ny, nz), 1)

    def copy_a(group, b):
        block = pl.ds(b * CHUNK, CHUNK)
        return pltpu.make_async_remote_copy(
            src_ref=send_a.at[group, :, block], dst_ref=recv_a.at[group, :, block],
            send_sem=a_send.at[group, b], recv_sem=a_recv.at[group, b],
            device_id={"shot": near}, device_id_type=MESH)

    def copy_b(b):
        block = pl.ds(b * CHUNK, CHUNK)
        return pltpu.make_async_remote_copy(
            src_ref=send_b.at[:, block], dst_ref=recv_b.at[:, block],
            send_sem=b_send.at[b], recv_sem=b_recv.at[b],
            device_id={"shot": far}, device_id_type=MESH)

    def correlate(b):
        r = b * CHUNK
        block = slice(REACH + r, REACH + r + CHUNK)
        for k in range(offsets):
            h = k - half
            total = None
            for s in range(shots):
                source = buf[q, 2 * s, block]
                receiver = buf[q, 2 * s + 1, block]
                if h % ny:
                    source = pltpu.roll(source, h % ny, 1)
                    receiver = pltpu.roll(receiver, (-h) % ny, 1)
                total = source * receiver if total is None else total + source * receiver
            if h:
                total = jnp.where((y_index >= abs(h)) & (y_index < ny - abs(h)), total, 0.0)
            part[k, r : r + CHUNK] = total
        for group, device in ((0, near_far), (1, near)):
            for j in range(per_device):
                send_a[group, j, r : r + CHUNK] = part[perm[device * per_device + j], r : r + CHUNK]
            copy_a(group, b).start()

    def relay(b):
        r = b * CHUNK
        copy_a(0, b).wait_recv()
        for j in range(per_device):
            send_b[j, r : r + CHUNK] = (
                part[perm[far * per_device + j], r : r + CHUNK] + recv_a[0, j, r : r + CHUNK])
        copy_b(b).start()

    def finish(b):
        r = b * CHUNK
        copy_a(1, b).wait_recv()
        copy_b(b).wait_recv()
        for j in range(per_device):
            image[j, r : r + CHUNK] = (
                part[perm[me * per_device + j], r : r + CHUNK]
                + recv_a[1, j, r : r + CHUNK] + recv_b[j, r : r + CHUNK])
        block = pl.ds(r, CHUNK)
        pltpu.make_async_copy(image.at[:, block], image_out.at[:, block], out_sem.at[b]).start()

    blocks = rows // CHUNK
    inner = list(range(1, blocks - 1))
    outer = [0, blocks - 1]
    for w in range(fields):
        side_terms(p, w)
        for b in inner:
            advance(p, q, w, b * CHUNK)
    for b in inner:
        correlate(b)
    for b in inner:
        relay(b)
    stores = []
    for w in range(fields):
        wait_low(p, w)
        advance(p, q, w, 0)
        wait_high(p, w)
        advance(p, q, w, rows - CHUNK)
        out = (source_out, receiver_out)[w % 2]
        stores.append(pltpu.make_async_copy(buf.at[q, w, body_rows], out.at[w // 2], out_sem.at[blocks + w]))
        stores[-1].start()
    for b in outer:
        correlate(b)
    for b in outer:
        relay(b)
    for b in inner + outer:
        finish(b)
    for b in range(blocks):
        copy_a(0, b).wait_send()
        copy_a(1, b).wait_send()
        copy_b(b).wait_send()
        block = pl.ds(b * CHUNK, CHUNK)
        pltpu.make_async_copy(image.at[:, block], image_out.at[:, block], out_sem.at[b]).wait()
    for store in stores:
        store.wait()


def store_kernel(image, source, receiver, image_out, source_out, receiver_out, held, load_sem, store_sem):
    pairs = ((image, image_out), (source, source_out), (receiver, receiver_out))
    moves = []
    for i, (value, out) in enumerate(pairs):
        for j in range(value.shape[0]):
            load = pltpu.make_async_copy(value.at[j], held.at[i, j], load_sem.at[i, j])
            store = pltpu.make_async_copy(held.at[i, j], out.at[j], store_sem.at[i, j])
            moves.append((load, store))
    for load, _ in moves:
        load.start()
    for load, store in moves:
        load.wait()
        store.start()
    for _, store in moves:
        store.wait()


def body(
    source_now, source_prev, receiver_now, receiver_prev, courant_sq, source_cell, wavelet,
    receiver_cell, traces, offset_perm,
):
    shots, rows, ny, nz = source_now.shape
    fields = 2 * shots
    cells = rows * ny
    offsets = offset_perm.shape[0]
    per_device = offsets // lax.axis_size("shot")
    blocks = rows // CHUNK
    anywhere = pl.BlockSpec(memory_space=pl.ANY)
    main = pl.BlockSpec(memory_space=pltpu.HBM)
    vector = pl.BlockSpec(memory_space=pltpu.VMEM)
    scalar = pl.BlockSpec(memory_space=pltpu.SMEM)
    f32 = jnp.float32
    field = jax.ShapeDtypeStruct(source_now.shape, f32)
    images = jax.ShapeDtypeStruct((per_device, rows, ny, nz), f32)
    results = pl.pallas_call(
        kernel,
        out_shape=(images, field, field),
        in_specs=[main] * 5 + [scalar, scalar, vector, main, scalar],
        out_specs=(anywhere,) * 3,
        scratch_shapes=[
            pltpu.VMEM((2, fields, rows + 2 * REACH, ny, nz), f32),
            pltpu.VMEM((rows, ny, nz), f32),
            pltpu.VMEM((fields, rows, ny, nz), f32),
            pltpu.VMEM((fields, cells, LANES), f32),
            pltpu.VMEM((LANES, receiver_cell.shape[1]), f32),
            pltpu.VMEM((nz, nz), jnp.bfloat16),
            pltpu.VMEM((nz, nz), jnp.bfloat16),
            pltpu.VMEM((cells, cells), jnp.bfloat16),
            pltpu.VMEM((cells, cells), jnp.bfloat16),
            pltpu.VMEM((offsets, rows, ny, nz), f32),
            pltpu.VMEM((2, per_device, rows, ny, nz), f32),
            pltpu.VMEM((2, per_device, rows, ny, nz), f32),
            pltpu.VMEM((per_device, rows, ny, nz), f32),
            pltpu.VMEM((per_device, rows, ny, nz), f32),
            pltpu.VMEM((per_device, rows, ny, nz), f32),
            pltpu.VMEM(traces.shape, f32),
            pltpu.SemaphoreType.DMA((2 * fields + 2,)),
            pltpu.SemaphoreType.DMA((fields, 2)),
            pltpu.SemaphoreType.DMA((2, fields, 2)),
            pltpu.SemaphoreType.DMA((2, blocks)),
            pltpu.SemaphoreType.DMA((2, blocks)),
            pltpu.SemaphoreType.DMA((blocks,)),
            pltpu.SemaphoreType.DMA((blocks,)),
            pltpu.SemaphoreType.DMA((blocks + fields,)),
        ],
        compiler_params=pltpu.CompilerParams(
            collective_id=0, has_side_effects=True, vmem_limit_bytes=GRANT
        ),
    )(
        source_now, source_prev, receiver_now, receiver_prev, courant_sq, source_cell, wavelet.T,
        receiver_cell, traces, offset_perm,
    )
    return pl.pallas_call(
        store_kernel,
        out_shape=(images, field, field),
        in_specs=[anywhere] * 3,
        out_specs=(main,) * 3,
        scratch_shapes=[
            pltpu.VMEM((3, max(shots, per_device), rows, ny, nz), f32),
            pltpu.SemaphoreType.DMA((3, max(shots, per_device))),
            pltpu.SemaphoreType.DMA((3, max(shots, per_device))),
        ],
        compiler_params=pltpu.CompilerParams(vmem_limit_bytes=GRANT),
    )(*results)


def solution(mesh):
    field = P(("runs", "shot"), "slab", None, None)
    in_specs = (
        field, field, field, field,
        P(("runs", "slab"), None, None),
        P(("runs", "shot")),
        P(None, ("runs", "shot")),
        P(("runs", "shot"), None),
        P(None, ("runs", "shot"), None),
        P("runs"),
    )
    return jax.shard_map(body, mesh=mesh, in_specs=in_specs, out_specs=(field,) * 3, check_vma=False)
```
